512 devices in a mesh: dp: 64 (over y, z_lo, core), blk: 8 (over z_hi, x).
Axes of the slice: x: 4, y: 4, z: 16 (z_hi: 2, z_lo: 8; z = z_hi * 8 + z_lo), core: 2. Of those that a mesh axis runs over, the one named last changes fastest.
Arguments:
- images: float32 [65536, 1152], P(('dp', 'blk')), may hold values from -12 to 12
- texts: float32 [65536, 1152], P(('dp', 'blk')), may hold values from -6 to 6
- positives: int32 [65536], P(('dp', 'blk')), may hold values from 0 to 127, as said below
- plan: int32 [3, 64], replicated, may hold values from 0 to 63, as said below
Outputs:
- image_grad: float32 [65536, 1152], P(('dp', 'blk'))
- text_grad: float32 [65536, 1152], P(('dp', 'blk'))
- totals: float32 [3], replicated
The draws below stay inside these ranges and needn't reach their ends.
Inputs may be any that keep to these rules, and one draw needn't show every extreme that they name: Within each device's block of 128 rows, positives holds every number 0 to 127 once. Each row of plan pairs the indices of dp: plan[r, plan[r, a]] = a and plan[r, a] != a. No two rounds pair the same two indices.
All inputs are finite; a program needn't handle non-finite values.
Results may differ from the reference program's by a relative error of at most 0.005.
Values may be sent and summed in bfloat16 or wider, within the bound.
A program may use at most 64 MiB of HBM per device.

```python
import math
import jax
import jax.numpy as jnp
from jax import lax

D = 1152
ROWS = 128
ROUNDS = 3
BATCH = 65536
N_DP = 64
N_BLK = 8


def draw_images(key, part):
    key = jax.random.fold_in(key, 5)
    ramp = 0.6 * jnp.exp(math.log(3.0) * jnp.arange(BATCH, dtype=jnp.float32) / (BATCH - 1))
    base = jnp.clip(jax.random.normal(key, (BATCH, D), jnp.float32), -4.0, 4.0)
    return (base * ramp[:, None]).astype(jnp.float32)


def draw_positives(key, part):
    key = jax.random.fold_in(key, 7)
    blocks = BATCH // ROWS
    scores = jax.random.randint(key, (blocks, ROWS), 0, 2 ** 20, dtype=jnp.int32) * ROWS + jnp.arange(ROWS, dtype=jnp.int32)[None, :]
    return jnp.argsort(scores, axis=1).astype(jnp.int32).reshape(BATCH)


def draw_plan(key, part):
    key = jax.random.fold_in(key, 11)
    first_key, second_key = jax.random.split(key)
    circle = N_DP - 1
    picks = jnp.argsort(jax.random.randint(first_key, (circle,), 0, 2 ** 20, dtype=jnp.int32) * circle + jnp.arange(circle, dtype=jnp.int32))[:ROUNDS].astype(jnp.int32)
    target_signs = jnp.argsort(jax.random.randint(second_key, (N_DP,), 0, 2 ** 20, dtype=jnp.int32) * N_DP + jnp.arange(N_DP, dtype=jnp.int32)).astype(jnp.int32)
    seats = jnp.arange(circle, dtype=jnp.int32)

    def one_round(pick):
        mirror = (2 * pick - seats) % circle
        mate = jnp.where(mirror == seats, circle, mirror).astype(jnp.int32)
        whole = jnp.concatenate([mate, pick[None]]).astype(jnp.int32)
        return jnp.zeros((N_DP,), jnp.int32).at[target_signs].set(target_signs[whole])
    return jax.vmap(one_round)(picks).astype(jnp.int32)


def level_of(own_key, extent, cuts, low, high):
    loudness, own = 1.0, jax.random.fold_in(own_key, 6)
    for axis_at, shards_of in cuts:
        steps = jnp.exp(jax.random.uniform(jax.random.fold_in(own, axis_at), (shards_of,), jnp.float32, low / len(cuts), high / len(cuts)))
        loudness = loudness * jnp.repeat(steps, extent[axis_at] // shards_of).reshape([-1 if axis == axis_at else 1 for axis in range(len(extent))])
    return loudness


def scatter_about(own_key, shape, deviation, bound, pieces=(), kind=jnp.bfloat16):
    gain = level_of(own_key, shape, pieces, -0.22, 0.18) if pieces else 1.0
    result = jax.random.normal(own_key, shape, jnp.float32) * deviation * gain
    return jnp.minimum(jnp.maximum(result, -bound), bound).astype(kind)


def setup_inputs(seed: int = 0) -> dict:
    keys = jax.random.split(jax.random.key(seed), 5)
    return {
        "images": draw_images(jax.random.fold_in(keys[4], 71), 0),
        "texts": scatter_about(keys[1], (BATCH, D), 1.0, 6.0, ((0, 512),), jnp.float32),
        "positives": draw_positives(jax.random.fold_in(keys[4], 71), 0),
        "plan": draw_plan(jax.random.fold_in(keys[4], 71), 0),
    }


LOGIT_SHARPNESS = 2.0
LOGIT_OFFSET = -2.0

def similarity(left, right, scale_factor):
    return lax.dot_general(left, right, (((1,), (1,)), ((), ())), preferred_element_type=jnp.float32) * scale_factor

def pair_terms(similarity_matrix, target_signs):
    pair_logits = LOGIT_SHARPNESS * similarity_matrix + LOGIT_OFFSET
    weights = jax.nn.sigmoid(pair_logits) - target_signs
    losses = jax.nn.softplus(pair_logits) - target_signs * pair_logits
    stats = jnp.stack([jnp.sum(losses), jnp.sum(weights), jnp.sum(weights * similarity_matrix)])
    return (weights.astype(jnp.bfloat16), stats)

def row_sum(weights, other):
    return jnp.dot(weights, other, preferred_element_type=jnp.float32)

def column_sum(weights, other):
    return lax.dot_general(weights, other, (((0,), (0,)), ((), ())), preferred_element_type=jnp.float32)

def reference(images, texts, positives, plan):
    left_all = images.astype(jnp.bfloat16)
    right_all = texts.astype(jnp.bfloat16)
    scale_factor = 1.0 / math.sqrt(D)
    gradient_factor = LOGIT_SHARPNESS * scale_factor

    def one_block(index):
        start = index * ROWS
        left = lax.dynamic_slice_in_dim(left_all, start, ROWS, 0)
        right = lax.dynamic_slice_in_dim(right_all, start, ROWS, 0)
        matches = lax.dynamic_slice_in_dim(positives, start, ROWS, 0)
        target_signs = (jnp.arange(ROWS, dtype=jnp.int32)[None, :] == matches[:, None]).astype(jnp.float32)
        weights, stats = pair_terms(similarity(left, right, scale_factor), target_signs)
        image_acc = row_sum(weights, right)
        text_gradient_total = column_sum(weights, left)
        for step in range(ROUNDS):
            other = ((plan[step, index // N_BLK] * N_BLK + index % N_BLK) * ROWS).astype(jnp.int32)
            their_left = lax.dynamic_slice_in_dim(left_all, other, ROWS, 0)
            their_right = lax.dynamic_slice_in_dim(right_all, other, ROWS, 0)
            forward, extra = pair_terms(similarity(left, their_right, scale_factor), 0.0)
            stats = stats + extra
            image_acc = image_acc + row_sum(forward, their_right)
            mirrored, unused = pair_terms(similarity(their_left, right, scale_factor), 0.0)
            text_gradient_total = text_gradient_total + column_sum(mirrored, their_left)
        return (image_acc * gradient_factor, text_gradient_total * gradient_factor, stats)
    blocks = jnp.arange(N_DP * N_BLK, dtype=jnp.int32)
    image_parts, text_parts, stat_parts = lax.map(one_block, blocks)
    pairs = float(BATCH * ROWS * (ROUNDS + 1))
    totals = lax.optimization_barrier(jnp.sum(stat_parts, axis=0)) / pairs
    return (image_parts.reshape(BATCH, D), text_parts.reshape(BATCH, D), totals)
```

```python
import functools
import math

import jax
import jax.numpy as jnp
from jax import lax
from jax.experimental import pallas as pl
from jax.experimental.pallas import tpu as pltpu
from jax.sharding import PartitionSpec as P

MESH = pl.DeviceIdType.MESH
LOGIT_SHARPNESS = 2.0
LOGIT_OFFSET = -2.0

ROUNDS = 3
CHIPS = 32
PIECES = 16
CHUNKS = 3


def terms(s):
    logit = LOGIT_SHARPNESS * s + LOGIT_OFFSET
    e = jnp.exp(-jnp.abs(logit))
    weight = jnp.where(logit >= 0.0, 1.0, e) / (1.0 + e)
    loss = jnp.maximum(logit, 0.0) + jnp.log1p(e)
    return logit, weight, loss


def nt(a, b):
    return lax.dot_general(a, b, (((1,), (1,)), ((), ())), preferred_element_type=jnp.float32)


def nn(a, b):
    return jnp.dot(a, b, preferred_element_type=jnp.float32)


def wait_bytes(ref, sem):
    pltpu.make_async_copy(ref, ref, sem).wait()


def kernel(
    pairs,
    images, texts, pos_col, pos_row, plan,
    image_grad, text_grad, totals,
    own, rr0, rr1, rr2, stg, arr, stat, red1, red2,
    send1, recv1, sends, recvs, send2, recv2, sendr, recvr,
):
    rr = (rr0, rr1, rr2)
    rows, width = images.shape
    cw = width // CHUNKS
    half_pieces = PIECES // 2
    scale = 1.0 / math.sqrt(width)
    factor = LOGIT_SHARPNESS * scale

    dp = lax.axis_index("dp")
    blk = lax.axis_index("blk")
    core = lax.rem(dp, 2)
    chip = dp // 2
    y, z = chip // 8, lax.rem(chip, 8)
    half = z // 4
    place = y * 4 + lax.rem(z, 4)

    def peer_chip(i):
        return chip ^ i

    def piece_of(t):
        return (t // 8) * 4 + lax.rem(t, 4)

    def mask_in_half(m):
        return (m // 4) * 8 + lax.rem(m, 4)

    def other(i):
        return dp ^ (i // 8), blk ^ lax.rem(i, 8)

    barrier = pltpu.get_barrier_semaphore()

    def greet(i, carry):
        pl.semaphore_signal(barrier, inc=1, device_id=(2 * peer_chip(i) + core, blk), device_id_type=MESH)
        return carry

    lax.fori_loop(1, CHIPS, greet, 0)

    def greet_other(i, carry):
        pl.semaphore_signal(barrier, inc=1, device_id=other(i), device_id_type=MESH)
        return carry

    lax.fori_loop(1, 16, greet_other, 0)

    for c in range(CHUNKS):
        for j in range(half_pieces):
            at = (slice(16 * j, 16 * j + 16), slice(c * cw, (c + 1) * cw))
            own[c, j] = images[at].astype(jnp.bfloat16)
            own[c, half_pieces + j] = texts[at].astype(jnp.bfloat16)
    for c in range(CHUNKS):
        rr[c][core, chip] = own[c, place]

    pl.semaphore_wait(barrier, CHIPS - 1 + 15)

    for c in range(CHUNKS):

        def spread(i, carry, c=c):
            t = peer_chip(i)
            pltpu.make_async_remote_copy(
                src_ref=own.at[c, piece_of(t)],
                dst_ref=rr[c].at[core, chip],
                send_sem=send1.at[c],
                recv_sem=recv1.at[c],
                device_id=(2 * t + core, blk),
                device_id_type=MESH,
            ).start()
            return carry

        lax.fori_loop(1, CHIPS, spread, 0)

    def x_own(c):
        return own[c, :half_pieces].reshape(rows, cw)

    def y_own(c):
        return own[c, half_pieces:].reshape(rows, cw)

    def x_their(c, r):
        return arr[c, :half_pieces, r].reshape(rows, cw)

    def y_their(c, r):
        return arr[c, half_pieces:, r].reshape(rows, cw)

    s = jnp.zeros((rows, rows), jnp.float32)
    st = jnp.zeros((rows, rows), jnp.float32)
    for c in range(CHUNKS):
        s = s + nt(x_own(c), y_own(c))
        st = st + nt(y_own(c), x_own(c))
    s = s * scale
    label = (lax.broadcasted_iota(jnp.int32, (rows, rows), 1) == pos_col[...]).astype(jnp.float32)
    label_t = (lax.broadcasted_iota(jnp.int32, (rows, rows), 0) == pos_row[...]).astype(jnp.float32)
    logit, weight, loss = terms(s)
    weight = weight - label
    loss_sum = loss - label * logit
    weight_sum = weight
    product_sum = weight * s
    weight_b = weight.astype(jnp.bfloat16)
    weight_t = (terms(st * scale)[1] - label_t).astype(jnp.bfloat16)
    for c in range(CHUNKS):
        at = slice(c * cw, (c + 1) * cw)
        image_grad[:, at] = nn(weight_b, y_own(c))
        text_grad[:, at] = nn(weight_t, x_own(c))

    for c in range(CHUNKS):
        wait_bytes(rr[c].at[0, pl.ds(0, CHIPS - 1)], recv1.at[c])
        share = pltpu.make_async_remote_copy(
            src_ref=rr[c].at[core],
            dst_ref=rr[c].at[core],
            send_sem=sends.at[c],
            recv_sem=recvs.at[c],
            device_id=(dp ^ 1, blk),
            device_id_type=MESH,
        )
        share.start()
        share.wait_recv()

        for r in range(ROUNDS):
            p = plan[r, dp]
            arr[c, place, r] = rr[c][lax.rem(p, 2), p // 2]

        def deliver(m, carry, c=c):
            t = peer_chip(mask_in_half(m))
            for r in range(ROUNDS):
                p = plan[r, 2 * t + core]
                stg[c, m, r] = rr[c][lax.rem(p, 2), p // 2]
            pltpu.make_async_remote_copy(
                src_ref=stg.at[c, m],
                dst_ref=arr.at[c, place],
                send_sem=send2.at[c],
                recv_sem=recv2.at[c],
                device_id=(2 * t + core, blk),
                device_id_type=MESH,
            ).start()
            return carry

        lax.fori_loop(1, PIECES, deliver, 0)

    ours = [jnp.zeros((rows, rows), jnp.float32) for _ in range(ROUNDS)]
    theirs = [jnp.zeros((rows, rows), jnp.float32) for _ in range(ROUNDS)]
    for c in range(CHUNKS):
        wait_bytes(arr.at[c, pl.ds(0, PIECES - 1)], recv2.at[c])
        for r in range(ROUNDS):
            ours[r] = ours[r] + nt(x_own(c), y_their(c, r))
            theirs[r] = theirs[r] + nt(y_own(c), x_their(c, r))
    forward, mirrored = [], []
    for r in range(ROUNDS):
        s = ours[r] * scale
        logit, weight, loss = terms(s)
        loss_sum = loss_sum + loss
        weight_sum = weight_sum + weight
        product_sum = product_sum + weight * s
        forward.append(weight.astype(jnp.bfloat16))
    rows_of = [jnp.sum(v, axis=0, keepdims=True) for v in (loss_sum, weight_sum, product_sum)]
    stat[...] = jnp.concatenate(rows_of + [jnp.zeros((5, rows), jnp.float32)], axis=0)

    def reduce_dp(i, carry):
        pltpu.make_async_remote_copy(
            src_ref=stat,
            dst_ref=red1.at[chip],
            send_sem=sendr.at[0],
            recv_sem=recvr.at[0],
            device_id=(2 * peer_chip(i) + core, blk),
            device_id_type=MESH,
        ).start()
        return carry

    lax.fori_loop(1, CHIPS, reduce_dp, 0)
    red1[chip] = stat[...]

    for r in range(ROUNDS):
        mirrored.append(terms(theirs[r] * scale)[1].astype(jnp.bfloat16))
    wait_bytes(red1.at[pl.ds(0, CHIPS - 1)], recvr.at[0])
    mine = 8 * core + blk
    red2[mine] = jnp.sum(red1[...], axis=0)

    def reduce_rest(i, carry):
        pltpu.make_async_remote_copy(
            src_ref=red2.at[mine],
            dst_ref=red2.at[mine],
            send_sem=sendr.at[1],
            recv_sem=recvr.at[1],
            device_id=other(i),
            device_id_type=MESH,
        ).start()
        return carry

    lax.fori_loop(1, 16, reduce_rest, 0)

    for c in range(CHUNKS):
        at = slice(c * cw, (c + 1) * cw)
        image_sum, text_sum = image_grad[:, at], text_grad[:, at]
        for r in range(ROUNDS):
            image_sum = image_sum + nn(forward[r], y_their(c, r))
            text_sum = text_sum + nn(mirrored[r], x_their(c, r))
        image_grad[:, at] = image_sum * factor
        text_grad[:, at] = text_sum * factor

    wait_bytes(red2.at[pl.ds(0, 15)], recvr.at[1])
    total = jnp.sum(red2[...], axis=0)
    for k in range(3):
        totals[k] = jnp.sum(total[k : k + 1, :]) / pairs

    for c in range(CHUNKS):
        wait_bytes(rr[c].at[0, pl.ds(0, CHIPS - 1)], send1.at[c])
        wait_bytes(rr[c].at[0], sends.at[c])
        wait_bytes(arr.at[c, pl.ds(0, PIECES - 1)], send2.at[c])
    wait_bytes(red1.at[pl.ds(0, CHIPS - 1)], sendr.at[0])
    wait_bytes(red2.at[pl.ds(0, 15)], sendr.at[1])


def body(images, texts, positives, plan):
    rows, width = images.shape
    rounds = plan.shape[0]
    pairs = float(rows * rows * (rounds + 1) * lax.axis_size("dp") * lax.axis_size("blk"))
    cw = width // CHUNKS
    vmem = pl.BlockSpec(memory_space=pltpu.VMEM)
    smem = pl.BlockSpec(memory_space=pltpu.SMEM)
    dma = pltpu.SemaphoreType.DMA
    return pl.pallas_call(
        functools.partial(kernel, pairs),
        out_shape=(
            jax.ShapeDtypeStruct((rows, width), jnp.float32),
            jax.ShapeDtypeStruct((rows, width), jnp.float32),
            jax.ShapeDtypeStruct((3,), jnp.float32),
        ),
        in_specs=[vmem, vmem, vmem, vmem, smem],
        out_specs=(vmem, vmem, smem),
        scratch_shapes=[
            pltpu.VMEM((CHUNKS, PIECES, 16, cw), jnp.bfloat16),
            *[pltpu.VMEM((2, CHIPS, 16, cw), jnp.bfloat16) for _ in range(CHUNKS)],
            pltpu.VMEM((CHUNKS, PIECES, ROUNDS, 16, cw), jnp.bfloat16),
            pltpu.VMEM((CHUNKS, PIECES, ROUNDS, 16, cw), jnp.bfloat16),
            pltpu.VMEM((8, rows), jnp.float32),
            pltpu.VMEM((CHIPS, 8, rows), jnp.float32),
            pltpu.VMEM((16, 8, rows), jnp.float32),
            dma((CHUNKS,)), dma((CHUNKS,)),
            dma((CHUNKS,)), dma((CHUNKS,)),
            dma((CHUNKS,)), dma((CHUNKS,)),
            dma((2,)), dma((2,)),
        ],
        compiler_params=pltpu.CompilerParams(
            collective_id=0, has_side_effects=True, vmem_limit_bytes=32 * 1024 * 1024
        ),
        cost_estimate=pl.CostEstimate(flops=600_000_000, bytes_accessed=3_000_000, transcendentals=400_000),
    )(images, texts, positives.reshape(rows, 1), positives.reshape(1, rows), plan)


def solution(mesh):
    placed = (P(("dp", "blk"), None), P(("dp", "blk"), None), P(("dp", "blk")), P())
    return jax.shard_map(
        body,
        mesh=mesh,
        in_specs=placed,
        out_specs=(P(("dp", "blk"), None), P(("dp", "blk"), None), P()),
        check_vma=False,
    )
```

```python
import functools
import math

import jax
import jax.numpy as jnp
from jax import lax
from jax.experimental import pallas as pl
from jax.experimental.pallas import tpu as pltpu
from jax.sharding import PartitionSpec as P

MESH = pl.DeviceIdType.MESH
LOGIT_SHARPNESS = 2.0
LOGIT_OFFSET = -2.0

ROUNDS = 3
CHIPS = 32
PIECES = 16
LANES = 128
CHUNKS = 9
GROUPS = [("y", g) for g in range(9)] + [("x", g) for g in range(9)]


def terms(s):
    logit = LOGIT_SHARPNESS * s + LOGIT_OFFSET
    e = jnp.exp(-jnp.abs(logit))
    weight = jnp.where(logit >= 0.0, 1.0, e) / (1.0 + e)
    loss = jnp.maximum(logit, 0.0) + jnp.log1p(e)
    return logit, weight, loss


def nt(a, b):
    return lax.dot_general(a, b, (((1,), (1,)), ((), ())), preferred_element_type=jnp.float32)


def nn(a, b):
    return jnp.dot(a, b, preferred_element_type=jnp.float32)


def wait_bytes(ref, sem):
    pltpu.make_async_copy(ref, ref, sem).wait()


def kernel(pairs, images_hbm, texts_hbm, positives_hbm, plan_hbm, image_grad, text_grad, totals, *scratch):
    own, rr, stg, arr = (scratch[k * CHUNKS : (k + 1) * CHUNKS] for k in range(4))
    (
        images, texts, pos_row, plan, xb, yb, stat, red1, red2,
        load, send1, recv1, sends, recvs, send2, recv2, sendr, recvr,
    ) = scratch[4 * CHUNKS :]
    rows, width = images.shape
    row_groups = rows // 16
    scale = 1.0 / math.sqrt(width)
    factor = LOGIT_SHARPNESS * scale

    dp = lax.axis_index("dp")
    blk = lax.axis_index("blk")
    core = lax.rem(dp, 2)
    chip = dp // 2
    place = (chip // 8) * 4 + lax.rem(chip, 4)

    def piece_of(t):
        return (t // 8) * 4 + lax.rem(t, 4)

    def peer_in_half(m):
        return chip ^ ((m // 4) * 8 + lax.rem(m, 4))

    def other(i):
        return dp ^ (i // 8), blk ^ lax.rem(i, 8)

    loads = [
        pltpu.make_async_copy(source, target, load.at[k])
        for k, (source, target) in enumerate(
            [(texts_hbm, texts), (images_hbm, images), (plan_hbm, plan), (positives_hbm, pos_row)]
        )
    ]
    for copy in loads:
        copy.start()

    barrier = pltpu.get_barrier_semaphore()

    def greet(i, carry):
        pl.semaphore_signal(barrier, inc=1, device_id=(2 * (chip ^ i) + core, blk), device_id_type=MESH)
        return carry

    lax.fori_loop(1, CHIPS, greet, 0)

    def greet_other(i, carry):
        pl.semaphore_signal(barrier, inc=1, device_id=other(i), device_id_type=MESH)
        return carry

    lax.fori_loop(1, 16, greet_other, 0)

    loads[0].wait()
    yb[...] = texts[...].astype(jnp.bfloat16)
    loads[1].wait()
    xb[...] = images[...].astype(jnp.bfloat16)
    for position, (kind, g) in enumerate(GROUPS):
        source = yb if kind == "y" else xb
        c, side = position // 2, position % 2
        columns = source[:, g * LANES : (g + 1) * LANES]
        own[c][side * row_groups : (side + 1) * row_groups] = columns.reshape(row_groups, 16, LANES)
    for c in range(CHUNKS):
        rr[c][core, chip] = own[c][place]

    pl.semaphore_wait(barrier, CHIPS - 1 + 15)

    for c in range(CHUNKS):

        def spread(i, carry, c=c):
            t = chip ^ i
            pltpu.make_async_remote_copy(
                src_ref=own[c].at[piece_of(t)],
                dst_ref=rr[c].at[core, chip],
                send_sem=send1.at[c],
                recv_sem=recv1.at[c],
                device_id=(2 * t + core, blk),
                device_id_type=MESH,
            ).start()
            return carry

        lax.fori_loop(1, CHIPS, spread, 0)

    loads[3].wait()
    s = nt(xb[...], yb[...]) * scale
    label_t = (lax.broadcasted_iota(jnp.int32, (rows, rows), 0) == pos_row[...]).astype(jnp.float32)
    label = label_t.T
    logit, weight, loss = terms(s)
    weight = weight - label
    loss_sum = loss - label * logit
    weight_sum = weight
    product_sum = weight * s
    image_grad[...] = nn(weight.astype(jnp.bfloat16), yb[...])
    weight = terms(nt(yb[...], xb[...]) * scale)[1] - label_t
    text_grad[...] = nn(weight.astype(jnp.bfloat16), xb[...])

    loads[2].wait()
    for c in range(CHUNKS):
        wait_bytes(rr[c].at[0, pl.ds(0, CHIPS - 1)], recv1.at[c])
        share = pltpu.make_async_remote_copy(
            src_ref=rr[c].at[core],
            dst_ref=rr[c].at[core],
            send_sem=sends.at[c],
            recv_sem=recvs.at[c],
            device_id=(dp ^ 1, blk),
            device_id_type=MESH,
        )
        share.start()
        share.wait_recv()

        for r in range(ROUNDS):
            p = plan[r, dp]
            arr[c][place, r] = rr[c][lax.rem(p, 2), p // 2]

        def deliver(m, carry, c=c):
            t = peer_in_half(m)
            for r in range(ROUNDS):
                p = plan[r, 2 * t + core]
                stg[c][m, r] = rr[c][lax.rem(p, 2), p // 2]
            pltpu.make_async_remote_copy(
                src_ref=stg[c].at[m],
                dst_ref=arr[c].at[place],
                send_sem=send2.at[c],
                recv_sem=recv2.at[c],
                device_id=(2 * t + core, blk),
                device_id_type=MESH,
            ).start()
            return carry

        lax.fori_loop(1, PIECES, deliver, 0)

    def their(kind, g, r):
        position = GROUPS.index((kind, g))
        c, side = position // 2, position % 2
        return arr[c][side * row_groups : (side + 1) * row_groups, r].reshape(rows, LANES)

    def scores(kind, mine, waited):
        sums = [jnp.zeros((rows, rows), jnp.float32) for _ in range(ROUNDS)]
        for g in range(width // LANES):
            c = GROUPS.index((kind, g)) // 2
            if c not in waited:
                wait_bytes(arr[c].at[pl.ds(0, PIECES - 1)], recv2.at[c])
                waited.add(c)
            for r in range(ROUNDS):
                sums[r] = sums[r] + nt(mine[:, g * LANES : (g + 1) * LANES], their(kind, g, r))
        return sums

    waited = set()
    weights = []
    for s in scores("y", xb, waited):
        s = s * scale
        logit, weight, loss = terms(s)
        loss_sum = loss_sum + loss
        weight_sum = weight_sum + weight
        product_sum = product_sum + weight * s
        weights.append(weight.astype(jnp.bfloat16))
    sums = [jnp.sum(v, axis=0, keepdims=True) for v in (loss_sum, weight_sum, product_sum)]
    stat[...] = jnp.concatenate(sums + [jnp.zeros((5, rows), jnp.float32)], axis=0)

    def reduce_dp(i, carry):
        pltpu.make_async_remote_copy(
            src_ref=stat,
            dst_ref=red1.at[chip],
            send_sem=sendr.at[0],
            recv_sem=recvr.at[0],
            device_id=(2 * (chip ^ i) + core, blk),
            device_id_type=MESH,
        ).start()
        return carry

    lax.fori_loop(1, CHIPS, reduce_dp, 0)
    red1[chip] = stat[...]

    for g in range(width // LANES):
        at = slice(g * LANES, (g + 1) * LANES)
        image_sum = image_grad[:, at]
        for r in range(ROUNDS):
            image_sum = image_sum + nn(weights[r], their("y", g, r))
        image_grad[:, at] = image_sum * factor

    wait_bytes(red1.at[pl.ds(0, CHIPS - 1)], recvr.at[0])
    mine = 8 * core + blk
    red2[mine] = jnp.sum(red1[...], axis=0)

    def reduce_rest(i, carry):
        pltpu.make_async_remote_copy(
            src_ref=red2.at[mine],
            dst_ref=red2.at[mine],
            send_sem=sendr.at[1],
            recv_sem=recvr.at[1],
            device_id=other(i),
            device_id_type=MESH,
        ).start()
        return carry

    lax.fori_loop(1, 16, reduce_rest, 0)

    weights = [terms(s * scale)[1].astype(jnp.bfloat16) for s in scores("x", yb, waited)]
    for g in range(width // LANES):
        at = slice(g * LANES, (g + 1) * LANES)
        text_sum = text_grad[:, at]
        for r in range(ROUNDS):
            text_sum = text_sum + nn(weights[r], their("x", g, r))
        text_grad[:, at] = text_sum * factor

    wait_bytes(red2.at[pl.ds(0, 15)], recvr.at[1])
    total = jnp.sum(red2[...], axis=0)
    for k in range(3):
        totals[k] = jnp.sum(total[k : k + 1, :]) / pairs

    for c in range(CHUNKS):
        wait_bytes(rr[c].at[0, pl.ds(0, CHIPS - 1)], send1.at[c])
        wait_bytes(rr[c].at[0], sends.at[c])
        wait_bytes(arr[c].at[pl.ds(0, PIECES - 1)], send2.at[c])
    wait_bytes(red1.at[pl.ds(0, CHIPS - 1)], sendr.at[0])
    wait_bytes(red2.at[pl.ds(0, 15)], sendr.at[1])


def body(images, texts, positives, plan):
    rows, width = images.shape
    rounds = plan.shape[0]
    pairs = float(rows * rows * (rounds + 1) * lax.axis_size("dp") * lax.axis_size("blk"))
    vmem = pl.BlockSpec(memory_space=pltpu.VMEM)
    smem = pl.BlockSpec(memory_space=pltpu.SMEM)
    hbm = pl.BlockSpec(memory_space=pltpu.HBM)
    dma = pltpu.SemaphoreType.DMA
    sixteen, single = jnp.bfloat16, jnp.float32
    return pl.pallas_call(
        functools.partial(kernel, pairs),
        out_shape=(
            jax.ShapeDtypeStruct((rows, width), single),
            jax.ShapeDtypeStruct((rows, width), single),
            jax.ShapeDtypeStruct((3,), single),
        ),
        in_specs=[hbm, hbm, hbm, hbm],
        out_specs=(vmem, vmem, smem),
        scratch_shapes=[
            *[pltpu.VMEM((PIECES, 16, LANES), sixteen)] * CHUNKS,
            *[pltpu.VMEM((2, CHIPS, 16, LANES), sixteen)] * CHUNKS,
            *[pltpu.VMEM((PIECES, ROUNDS, 16, LANES), sixteen)] * CHUNKS,
            *[pltpu.VMEM((PIECES, ROUNDS, 16, LANES), sixteen)] * CHUNKS,
            pltpu.VMEM((rows, width), single),
            pltpu.VMEM((rows, width), single),
            pltpu.VMEM((1, rows), jnp.int32),
            pltpu.SMEM(plan.shape, jnp.int32),
            pltpu.VMEM((rows, width), sixteen),
            pltpu.VMEM((rows, width), sixteen),
            pltpu.VMEM((8, rows), single),
            pltpu.VMEM((CHIPS, 8, rows), single),
            pltpu.VMEM((16, 8, rows), single),
            dma((4,)),
            dma((CHUNKS,)), dma((CHUNKS,)),
            dma((CHUNKS,)), dma((CHUNKS,)),
            dma((CHUNKS,)), dma((CHUNKS,)),
            dma((2,)), dma((2,)),
        ],
        compiler_params=pltpu.CompilerParams(
            collective_id=0, has_side_effects=True, vmem_limit_bytes=32 * 1024 * 1024
        ),
        cost_estimate=pl.CostEstimate(flops=600_000_000, bytes_accessed=3_000_000, transcendentals=400_000),
    )(images, texts, positives.reshape(1, rows), plan)


def solution(mesh):
    placed = (P(("dp", "blk"), None), P(("dp", "blk"), None), P(("dp", "blk")), P())
    return jax.shard_map(
        body,
        mesh=mesh,
        in_specs=placed,
        out_specs=(P(("dp", "blk"), None), P(("dp", "blk"), None), P()),
        check_vma=False,
    )
```

```python
import functools
import math

import jax
import jax.numpy as jnp
from jax import lax
from jax.experimental import pallas as pl
from jax.experimental.pallas import tpu as pltpu
from jax.sharding import PartitionSpec as P

MESH = pl.DeviceIdType.MESH
LOGIT_SHARPNESS = 2.0
LOGIT_OFFSET = -2.0

ROUNDS = 3
CHIPS = 32
PIECES = 16
LANES = 128
CHUNKS = 9
FLIGHT = 3
TEXTS_AT = 4
SECOND_AT = 5
THIRD_AT = 6
GROUPS = [("y", g) for g in range(9)] + [("x", g) for g in range(9)]


def terms(s):
    logit = LOGIT_SHARPNESS * s + LOGIT_OFFSET
    e = jnp.exp(-jnp.abs(logit))
    weight = jnp.where(logit >= 0.0, 1.0, e) / (1.0 + e)
    loss = jnp.maximum(logit, 0.0) + jnp.log1p(e)
    return logit, weight, loss


def nt(a, b):
    return lax.dot_general(a, b, (((1,), (1,)), ((), ())), preferred_element_type=jnp.float32)


def nn(a, b):
    return jnp.dot(a, b, preferred_element_type=jnp.float32)


def wait_bytes(ref, sem):
    pltpu.make_async_copy(ref, ref, sem).wait()


def kernel(pairs, images_hbm, texts_hbm, positives_hbm, plan_hbm, image_grad, text_grad, totals, *scratch):
    own, rr, stg, arr = (scratch[k * CHUNKS : (k + 1) * CHUNKS] for k in range(4))
    (
        images, texts, pos_row, plan, xb, yb, stat, stat_z, stat_core, stat_sibling, red1, red2,
        load, send1, recv1, sends, recvs, send2, recv2, sendr, recvr,
    ) = scratch[4 * CHUNKS :]
    rows, width = images.shape
    row_groups = rows // 16
    scale = 1.0 / math.sqrt(width)
    factor = LOGIT_SHARPNESS * scale

    dp = lax.axis_index("dp")
    blk = lax.axis_index("blk")
    core = lax.rem(dp, 2)
    chip = dp // 2
    place = (chip // 8) * 4 + lax.rem(chip, 4)

    def piece_of(t):
        return (t // 8) * 4 + lax.rem(t, 4)

    def peer_in_half(m):
        return chip ^ ((m // 4) * 8 + lax.rem(m, 4))

    def along_z(i):
        return dp ^ (2 * lax.rem(i, 8)), blk ^ (4 * (i // 8))

    def across(i):
        return dp ^ (16 * (i // 4)), blk ^ lax.rem(i, 4)

    loads = [
        pltpu.make_async_copy(source, target, load.at[k])
        for k, (source, target) in enumerate(
            [(texts_hbm, texts), (images_hbm, images), (plan_hbm, plan), (positives_hbm, pos_row)]
        )
    ]
    for copy in loads:
        copy.start()

    barrier = pltpu.get_barrier_semaphore()

    def greet(i, carry):
        pl.semaphore_signal(barrier, inc=1, device_id=(2 * (chip ^ i) + core, blk), device_id_type=MESH)
        return carry

    lax.fori_loop(1, CHIPS, greet, 0)

    pl.semaphore_signal(barrier, inc=1, device_id=(dp ^ 1, blk), device_id_type=MESH)

    def greet_z(i, carry):
        pl.semaphore_signal(barrier, inc=1, device_id=along_z(i), device_id_type=MESH)
        return carry

    lax.fori_loop(8, 16, greet_z, 0)

    def greet_across(i, carry):
        other = across((i // 3) * 4 + lax.rem(i, 3) + 1)
        pl.semaphore_signal(barrier, inc=1, device_id=other, device_id_type=MESH)
        return carry

    lax.fori_loop(0, 12, greet_across, 0)

    loads[0].wait()
    yb[...] = texts[...].astype(jnp.bfloat16)
    loads[1].wait()
    xb[...] = images[...].astype(jnp.bfloat16)
    for position, (kind, g) in enumerate(GROUPS):
        source = yb if kind == "y" else xb
        c, side = position // 2, position % 2
        columns = source[:, g * LANES : (g + 1) * LANES]
        own[c][side * row_groups : (side + 1) * row_groups] = columns.reshape(row_groups, 16, LANES)
    for c in range(CHUNKS):
        rr[c][core, chip] = own[c][place]

    pl.semaphore_wait(barrier, CHIPS + 8 + 12)

    def spread(c):
        def send(i, carry):
            t = chip ^ i
            pltpu.make_async_remote_copy(
                src_ref=own[c].at[piece_of(t)],
                dst_ref=rr[c].at[core, chip],
                send_sem=send1.at[c],
                recv_sem=recv1.at[c],
                device_id=(2 * t + core, blk),
                device_id_type=MESH,
            ).start()
            return carry

        lax.fori_loop(1, CHIPS, send, 0)

    for c in range(FLIGHT):
        spread(c)

    loads[3].wait()
    s = nt(xb[...], yb[...]) * scale
    label_t = (lax.broadcasted_iota(jnp.int32, (rows, rows), 0) == pos_row[...]).astype(jnp.float32)
    label = label_t.T
    logit, weight, loss = terms(s)
    weight = weight - label
    loss_sum = loss - label * logit
    weight_sum = weight
    product_sum = weight * s
    image_grad[...] = nn(weight.astype(jnp.bfloat16), yb[...])
    weight = terms(nt(yb[...], xb[...]) * scale)[1] - label_t
    text_grad[...] = nn(weight.astype(jnp.bfloat16), xb[...])

    def deliver(c):
        wait_bytes(rr[c].at[0, pl.ds(0, CHIPS - 1)], recv1.at[c])
        share = pltpu.make_async_remote_copy(
            src_ref=rr[c].at[core],
            dst_ref=rr[c].at[core],
            send_sem=sends.at[c],
            recv_sem=recvs.at[c],
            device_id=(dp ^ 1, blk),
            device_id_type=MESH,
        )
        share.start()
        share.wait_recv()

        for r in range(ROUNDS):
            p = plan[r, dp]
            arr[c][place, r] = rr[c][lax.rem(p, 2), p // 2]

        def send(m, carry):
            t = peer_in_half(m)
            for r in range(ROUNDS):
                p = plan[r, 2 * t + core]
                stg[c][m, r] = rr[c][lax.rem(p, 2), p // 2]
            pltpu.make_async_remote_copy(
                src_ref=stg[c].at[m],
                dst_ref=arr[c].at[place],
                send_sem=send2.at[c],
                recv_sem=recv2.at[c],
                device_id=(2 * t + core, blk),
                device_id_type=MESH,
            ).start()
            return carry

        lax.fori_loop(1, PIECES, send, 0)
        if c + FLIGHT < CHUNKS:
            spread(c + FLIGHT)

    def their(kind, g, r):
        position = GROUPS.index((kind, g))
        c, side = position // 2, position % 2
        return arr[c][side * row_groups : (side + 1) * row_groups, r].reshape(rows, LANES)

    def scores(kind, mine, waited):
        sums = [jnp.zeros((rows, rows), jnp.float32) for _ in range(ROUNDS)]
        for g in range(width // LANES):
            c = GROUPS.index((kind, g)) // 2
            if c not in waited:
                wait_bytes(arr[c].at[pl.ds(0, PIECES - 1)], recv2.at[c])
                waited.add(c)
            for r in range(ROUNDS):
                sums[r] = sums[r] + nt(mine[:, g * LANES : (g + 1) * LANES], their(kind, g, r))
        return sums

    loads[2].wait()
    for c in range(TEXTS_AT + 1):
        deliver(c)

    waited = set()
    weights = []
    for s in scores("y", xb, waited):
        s = s * scale
        logit, weight, loss = terms(s)
        loss_sum = loss_sum + loss
        weight_sum = weight_sum + weight
        product_sum = product_sum + weight * s
        weights.append(weight.astype(jnp.bfloat16))
    lane = lax.broadcasted_iota(jnp.int32, (1, rows), 1)
    stat[...] = jnp.zeros((1, rows), jnp.float32)
    for k, v in enumerate((loss_sum, weight_sum, product_sum)):
        stat[...] += jnp.where(lane == k, jnp.sum(v), 0.0)

    def exchange(k, source, slots, at, peer):
        slots[at] = source[...]

        def send(i, carry):
            pltpu.make_async_remote_copy(
                src_ref=source,
                dst_ref=slots.at[at],
                send_sem=sendr.at[k],
                recv_sem=recvr.at[k],
                device_id=peer(i),
                device_id_type=MESH,
            ).start()
            return carry

        lax.fori_loop(1, 16, send, 0)

    exchange(0, stat, red1, (blk // 4) * 8 + lax.rem(chip, 8), along_z)
    for c in range(TEXTS_AT + 1, SECOND_AT + 1):
        deliver(c)

    wait_bytes(red1.at[pl.ds(0, 15)], recvr.at[0])
    stat_z[...] = jnp.sum(red1[...], axis=0)
    exchange(1, stat_z, red2, (chip // 8) * 4 + lax.rem(blk, 4), across)
    for c in range(SECOND_AT + 1, THIRD_AT + 1):
        deliver(c)

    wait_bytes(red2.at[pl.ds(0, 15)], recvr.at[1])
    stat_core[...] = jnp.sum(red2[...], axis=0)
    swap = pltpu.make_async_remote_copy(
        src_ref=stat_core,
        dst_ref=stat_sibling,
        send_sem=sendr.at[2],
        recv_sem=recvr.at[2],
        device_id=(dp ^ 1, blk),
        device_id_type=MESH,
    )
    swap.start()
    for c in range(THIRD_AT + 1, CHUNKS):
        deliver(c)

    for g in range(width // LANES):
        at = slice(g * LANES, (g + 1) * LANES)
        image_sum = image_grad[:, at]
        for r in range(ROUNDS):
            image_sum = image_sum + nn(weights[r], their("y", g, r))
        image_grad[:, at] = image_sum * factor

    weights = [terms(s * scale)[1].astype(jnp.bfloat16) for s in scores("x", yb, waited)]
    for g in range(width // LANES):
        at = slice(g * LANES, (g + 1) * LANES)
        text_sum = text_grad[:, at]
        for r in range(ROUNDS):
            text_sum = text_sum + nn(weights[r], their("x", g, r))
        text_grad[:, at] = text_sum * factor

    swap.wait_recv()
    total = stat_core[...] + stat_sibling[...]
    for k in range(3):
        totals[k] = jnp.sum(jnp.where(lane == k, total, 0.0)) / pairs

    for c in range(CHUNKS):
        wait_bytes(rr[c].at[0, pl.ds(0, CHIPS - 1)], send1.at[c])
        wait_bytes(rr[c].at[0], sends.at[c])
        wait_bytes(arr[c].at[pl.ds(0, PIECES - 1)], send2.at[c])
    wait_bytes(red1.at[pl.ds(0, 15)], sendr.at[0])
    wait_bytes(red2.at[pl.ds(0, 15)], sendr.at[1])
    swap.wait_send()


def body(images, texts, positives, plan):
    rows, width = images.shape
    rounds = plan.shape[0]
    pairs = float(rows * rows * (rounds + 1) * lax.axis_size("dp") * lax.axis_size("blk"))
    vmem = pl.BlockSpec(memory_space=pltpu.VMEM)
    smem = pl.BlockSpec(memory_space=pltpu.SMEM)
    hbm = pl.BlockSpec(memory_space=pltpu.HBM)
    dma = pltpu.SemaphoreType.DMA
    sixteen, single = jnp.bfloat16, jnp.float32
    return pl.pallas_call(
        functools.partial(kernel, pairs),
        out_shape=(
            jax.ShapeDtypeStruct((rows, width), single),
            jax.ShapeDtypeStruct((rows, width), single),
            jax.ShapeDtypeStruct((3,), single),
        ),
        in_specs=[hbm, hbm, hbm, hbm],
        out_specs=(vmem, vmem, smem),
        scratch_shapes=[
            *[pltpu.VMEM((PIECES, 16, LANES), sixteen)] * CHUNKS,
            *[pltpu.VMEM((2, CHIPS, 16, LANES), sixteen)] * CHUNKS,
            *[pltpu.VMEM((PIECES, ROUNDS, 16, LANES), sixteen)] * CHUNKS,
            *[pltpu.VMEM((PIECES, ROUNDS, 16, LANES), sixteen)] * CHUNKS,
            pltpu.VMEM((rows, width), single),
            pltpu.VMEM((rows, width), single),
            pltpu.VMEM((1, rows), jnp.int32),
            pltpu.SMEM(plan.shape, jnp.int32),
            pltpu.VMEM((rows, width), sixteen),
            pltpu.VMEM((rows, width), sixteen),
            *[pltpu.VMEM((1, rows), single)] * 4,
            *[pltpu.VMEM((16, 1, rows), single)] * 2,
            dma((4,)),
            dma((CHUNKS,)), dma((CHUNKS,)),
            dma((CHUNKS,)), dma((CHUNKS,)),
            dma((CHUNKS,)), dma((CHUNKS,)),
            dma((3,)), dma((3,)),
        ],
        compiler_params=pltpu.CompilerParams(
            collective_id=0, has_side_effects=True, vmem_limit_bytes=53 * 1024 * 1024
        ),
        cost_estimate=pl.CostEstimate(flops=600_000_000, bytes_accessed=3_000_000, transcendentals=400_000),
    )(images, texts, positives.reshape(1, rows), plan)


def solution(mesh):
    placed = (P(("dp", "blk"), None), P(("dp", "blk"), None), P(("dp", "blk")), P())
    return jax.shard_map(
        body,
        mesh=mesh,
        in_specs=placed,
        out_specs=(P(("dp", "blk"), None), P(("dp", "blk"), None), P()),
        check_vma=False,
    )
```

```python
import functools
import math

import jax
import jax.numpy as jnp
from jax import lax
from jax.experimental import pallas as pl
from jax.experimental.pallas import tpu as pltpu
from jax.sharding import PartitionSpec as P

MESH = pl.DeviceIdType.MESH
LOGIT_SHARPNESS = 2.0
LOGIT_OFFSET = -2.0

ROUNDS = 3
CHIPS = 32
PIECES = 16
LANES = 128
CHUNKS = 9
FLIGHT = 3
TEXTS_AT = 5
FIRST_AT = 5
SECOND_AT = 6
THIRD_AT = 7
GROUPS = [("y", g) for g in range(9)] + [("x", g) for g in range(9)]


def terms(s):
    logit = LOGIT_SHARPNESS * s + LOGIT_OFFSET
    e = jnp.exp(-jnp.abs(logit))
    weight = jnp.where(logit >= 0.0, 1.0, e) / (1.0 + e)
    loss = jnp.maximum(logit, 0.0) + jnp.log1p(e)
    return logit, weight, loss


def nt(a, b):
    return lax.dot_general(a, b, (((1,), (1,)), ((), ())), preferred_element_type=jnp.float32)


def nn(a, b):
    return jnp.dot(a, b, preferred_element_type=jnp.float32)


def wait_bytes(ref, sem):
    pltpu.make_async_copy(ref, ref, sem).wait()


def kernel(pairs, images_hbm, texts_hbm, positives_hbm, plan_hbm, image_grad, text_grad, totals, *scratch):
    own, rr, stg, arr = (scratch[k * CHUNKS : (k + 1) * CHUNKS] for k in range(4))
    (
        images, texts, pos_row, plan, xb, yb, stat, stat_z, stat_all, stat_sibling, red1, red2,
        load, send1, recv1, sends, recvs, send2, recv2, sendr, recvr, ready,
    ) = scratch[4 * CHUNKS :]
    rows, width = images.shape
    row_groups = rows // 16
    scale = 1.0 / math.sqrt(width)
    factor = LOGIT_SHARPNESS * scale

    dp = lax.axis_index("dp")
    blk = lax.axis_index("blk")
    core = lax.rem(dp, 2)
    chip = dp // 2
    place = (chip // 8) * 4 + lax.rem(chip, 4)

    def piece_of(t):
        return (t // 8) * 4 + lax.rem(t, 4)

    def peer_in_half(m):
        return chip ^ ((m // 4) * 8 + lax.rem(m, 4))

    def along_z(i):
        return dp ^ (2 * lax.rem(i, 8)), blk ^ (4 * (i // 8))

    def across(i):
        return dp ^ (16 * (i // 4)), blk ^ lax.rem(i, 4)

    loads = [
        pltpu.make_async_copy(source, target, load.at[k])
        for k, (source, target) in enumerate(
            [(texts_hbm, texts), (images_hbm, images), (plan_hbm, plan), (positives_hbm, pos_row)]
        )
    ]
    for copy in loads:
        copy.start()

    barrier = pltpu.get_barrier_semaphore()

    def greet(i, carry):
        pl.semaphore_signal(barrier, inc=1, device_id=(2 * (chip ^ i), blk), device_id_type=MESH)
        return carry

    lax.fori_loop(1, CHIPS, greet, 0)

    @pl.when(core == 1)
    def _():
        pl.semaphore_signal(barrier, inc=1, device_id=(dp ^ 1, blk), device_id_type=MESH)

        def greet_z(i, carry):
            pl.semaphore_signal(barrier, inc=1, device_id=along_z(i), device_id_type=MESH)
            return carry

        lax.fori_loop(8, 16, greet_z, 0)

        def greet_across(i, carry):
            other = across((i // 3) * 4 + lax.rem(i, 3) + 1)
            pl.semaphore_signal(barrier, inc=1, device_id=other, device_id_type=MESH)
            return carry

        lax.fori_loop(0, 12, greet_across, 0)

    loads[0].wait()
    yb[...] = texts[...].astype(jnp.bfloat16)
    loads[1].wait()
    xb[...] = images[...].astype(jnp.bfloat16)
    for position, (kind, g) in enumerate(GROUPS):
        source = yb if kind == "y" else xb
        c, side = position // 2, position % 2
        columns = source[:, g * LANES : (g + 1) * LANES]
        own[c][side * row_groups : (side + 1) * row_groups] = columns.reshape(row_groups, 16, LANES)
    for c in range(CHUNKS):
        rr[c][core, chip] = own[c][place]

    @pl.when(core == 0)
    def _():
        pl.semaphore_wait(barrier, 2 * CHIPS - 1)
        pl.semaphore_signal(ready, inc=1, device_id=(dp ^ 1, blk), device_id_type=MESH)

    @pl.when(core == 1)
    def _():
        pl.semaphore_wait(ready, 1)

    def spread(c):
        def send(i, carry):
            t = chip ^ i
            pltpu.make_async_remote_copy(
                src_ref=own[c].at[piece_of(t)],
                dst_ref=rr[c].at[core, chip],
                send_sem=send1.at[c],
                recv_sem=recv1.at[c],
                device_id=(2 * t + core, blk),
                device_id_type=MESH,
            ).start()
            return carry

        lax.fori_loop(1, CHIPS, send, 0)

    for c in range(FLIGHT):
        spread(c)

    loads[3].wait()
    s = nt(xb[...], yb[...]) * scale
    label_t = (lax.broadcasted_iota(jnp.int32, (rows, rows), 0) == pos_row[...]).astype(jnp.float32)
    label = label_t.T
    logit, weight, loss = terms(s)
    weight = weight - label
    loss_sum = loss - label * logit
    weight_sum = weight
    product_sum = weight * s
    image_grad[...] = nn(weight.astype(jnp.bfloat16), yb[...])
    weight = terms(nt(yb[...], xb[...]) * scale)[1] - label_t
    text_grad[...] = nn(weight.astype(jnp.bfloat16), xb[...])

    def deliver(c):
        wait_bytes(rr[c].at[0, pl.ds(0, CHIPS - 1)], recv1.at[c])
        share = pltpu.make_async_remote_copy(
            src_ref=rr[c].at[core],
            dst_ref=rr[c].at[core],
            send_sem=sends.at[c],
            recv_sem=recvs.at[c],
            device_id=(dp ^ 1, blk),
            device_id_type=MESH,
        )
        share.start()
        share.wait_recv()

        for r in range(ROUNDS):
            p = plan[r, dp]
            arr[c][place, r] = rr[c][lax.rem(p, 2), p // 2]

        def send(m, carry):
            t = peer_in_half(m)
            for r in range(ROUNDS):
                p = plan[r, 2 * t + core]
                stg[c][m, r] = rr[c][lax.rem(p, 2), p // 2]
            pltpu.make_async_remote_copy(
                src_ref=stg[c].at[m],
                dst_ref=arr[c].at[place],
                send_sem=send2.at[c],
                recv_sem=recv2.at[c],
                device_id=(2 * t + core, blk),
                device_id_type=MESH,
            ).start()
            return carry

        lax.fori_loop(1, PIECES, send, 0)
        if c + FLIGHT < CHUNKS:
            spread(c + FLIGHT)

    def their(kind, g, r):
        position = GROUPS.index((kind, g))
        c, side = position // 2, position % 2
        return arr[c][side * row_groups : (side + 1) * row_groups, r].reshape(rows, LANES)

    def scores(kind, mine, waited):
        sums = [jnp.zeros((rows, rows), jnp.float32) for _ in range(ROUNDS)]
        for g in range(width // LANES):
            c = GROUPS.index((kind, g)) // 2
            if c not in waited:
                wait_bytes(arr[c].at[pl.ds(0, PIECES - 1)], recv2.at[c])
                waited.add(c)
            for r in range(ROUNDS):
                sums[r] = sums[r] + nt(mine[:, g * LANES : (g + 1) * LANES], their(kind, g, r))
        return sums

    loads[2].wait()
    for c in range(TEXTS_AT + 1):
        deliver(c)

    waited = set()
    weights = []
    for s in scores("y", xb, waited):
        s = s * scale
        logit, weight, loss = terms(s)
        loss_sum = loss_sum + loss
        weight_sum = weight_sum + weight
        product_sum = product_sum + weight * s
        weights.append(weight.astype(jnp.bfloat16))
    lane = lax.broadcasted_iota(jnp.int32, (1, rows), 1)
    stat[...] = jnp.zeros((1, rows), jnp.float32)
    for k, v in enumerate((loss_sum, weight_sum, product_sum)):
        stat[...] += jnp.where(lane == k, jnp.sum(v), 0.0)

    def exchange(k, source, slots, at, peer):
        slots[at] = source[...]

        def send(i, carry):
            pltpu.make_async_remote_copy(
                src_ref=source,
                dst_ref=slots.at[at],
                send_sem=sendr.at[k],
                recv_sem=recvr.at[k],
                device_id=peer(i),
                device_id_type=MESH,
            ).start()
            return carry

        lax.fori_loop(1, 16, send, 0)

    def to_sibling(k, source):
        return pltpu.make_async_remote_copy(
            src_ref=source,
            dst_ref=stat_sibling,
            send_sem=sendr.at[k],
            recv_sem=recvr.at[k],
            device_id=(dp ^ 1, blk),
            device_id_type=MESH,
        )

    @pl.when(core == 0)
    def _():
        to_sibling(2, stat).start()

    for c in range(TEXTS_AT + 1, FIRST_AT + 1):
        deliver(c)

    @pl.when(core == 1)
    def _():
        to_sibling(2, stat).wait_recv()
        stat[...] += stat_sibling[...]
        pl.semaphore_wait(barrier, 8 + 12)
        exchange(0, stat, red1, (blk // 4) * 8 + lax.rem(chip, 8), along_z)

    for c in range(FIRST_AT + 1, SECOND_AT + 1):
        deliver(c)

    @pl.when(core == 1)
    def _():
        wait_bytes(red1.at[pl.ds(0, 15)], recvr.at[0])
        stat_z[...] = jnp.sum(red1[...], axis=0)
        exchange(1, stat_z, red2, (chip // 8) * 4 + lax.rem(blk, 4), across)

    for c in range(SECOND_AT + 1, THIRD_AT + 1):
        deliver(c)

    @pl.when(core == 1)
    def _():
        wait_bytes(red2.at[pl.ds(0, 15)], recvr.at[1])
        stat_all[...] = jnp.sum(red2[...], axis=0)
        stat_sibling[...] = stat_all[...]
        to_sibling(3, stat_all).start()

    for c in range(THIRD_AT + 1, CHUNKS):
        deliver(c)

    for g in range(width // LANES):
        at = slice(g * LANES, (g + 1) * LANES)
        image_sum = image_grad[:, at]
        for r in range(ROUNDS):
            image_sum = image_sum + nn(weights[r], their("y", g, r))
        image_grad[:, at] = image_sum * factor

    weights = [terms(s * scale)[1].astype(jnp.bfloat16) for s in scores("x", yb, waited)]
    for g in range(width // LANES):
        at = slice(g * LANES, (g + 1) * LANES)
        text_sum = text_grad[:, at]
        for r in range(ROUNDS):
            text_sum = text_sum + nn(weights[r], their("x", g, r))
        text_grad[:, at] = text_sum * factor

    @pl.when(core == 0)
    def _():
        to_sibling(3, stat_all).wait_recv()

    total = stat_sibling[...]
    for k in range(3):
        totals[k] = jnp.sum(jnp.where(lane == k, total, 0.0)) / pairs

    for c in range(CHUNKS):
        wait_bytes(rr[c].at[0, pl.ds(0, CHIPS - 1)], send1.at[c])
        wait_bytes(rr[c].at[0], sends.at[c])
        wait_bytes(arr[c].at[pl.ds(0, PIECES - 1)], send2.at[c])

    @pl.when(core == 0)
    def _():
        to_sibling(2, stat).wait_send()

    @pl.when(core == 1)
    def _():
        wait_bytes(red1.at[pl.ds(0, 15)], sendr.at[0])
        wait_bytes(red2.at[pl.ds(0, 15)], sendr.at[1])
        to_sibling(3, stat_all).wait_send()


def body(images, texts, positives, plan):
    rows, width = images.shape
    rounds = plan.shape[0]
    pairs = float(rows * rows * (rounds + 1) * lax.axis_size("dp") * lax.axis_size("blk"))
    vmem = pl.BlockSpec(memory_space=pltpu.VMEM)
    smem = pl.BlockSpec(memory_space=pltpu.SMEM)
    hbm = pl.BlockSpec(memory_space=pltpu.HBM)
    dma = pltpu.SemaphoreType.DMA
    sixteen, single = jnp.bfloat16, jnp.float32
    return pl.pallas_call(
        functools.partial(kernel, pairs),
        out_shape=(
            jax.ShapeDtypeStruct((rows, width), single),
            jax.ShapeDtypeStruct((rows, width), single),
            jax.ShapeDtypeStruct((3,), single),
        ),
        in_specs=[hbm, hbm, hbm, hbm],
        out_specs=(vmem, vmem, smem),
        scratch_shapes=[
            *[pltpu.VMEM((PIECES, 16, LANES), sixteen)] * CHUNKS,
            *[pltpu.VMEM((2, CHIPS, 16, LANES), sixteen)] * CHUNKS,
            *[pltpu.VMEM((PIECES, ROUNDS, 16, LANES), sixteen)] * CHUNKS,
            *[pltpu.VMEM((PIECES, ROUNDS, 16, LANES), sixteen)] * CHUNKS,
            pltpu.VMEM((rows, width), single),
            pltpu.VMEM((rows, width), single),
            pltpu.VMEM((1, rows), jnp.int32),
            pltpu.SMEM(plan.shape, jnp.int32),
            pltpu.VMEM((rows, width), sixteen),
            pltpu.VMEM((rows, width), sixteen),
            *[pltpu.VMEM((1, rows), single)] * 4,
            *[pltpu.VMEM((16, 1, rows), single)] * 2,
            dma((4,)),
            dma((CHUNKS,)), dma((CHUNKS,)),
            dma((CHUNKS,)), dma((CHUNKS,)),
            dma((CHUNKS,)), dma((CHUNKS,)),
            dma((4,)), dma((4,)),
            pltpu.SemaphoreType.REGULAR,
        ],
        compiler_params=pltpu.CompilerParams(
            collective_id=0, has_side_effects=True, vmem_limit_bytes=60 * 1024 * 1024
        ),
        cost_estimate=pl.CostEstimate(flops=600_000_000, bytes_accessed=3_000_000, transcendentals=400_000),
    )(images, texts, positives.reshape(1, rows), plan)


def solution(mesh):
    placed = (P(("dp", "blk"), None), P(("dp", "blk"), None), P(("dp", "blk")), P())
    return jax.shard_map(
        body,
        mesh=mesh,
        in_specs=placed,
        out_specs=(P(("dp", "blk"), None), P(("dp", "blk"), None), P()),
        check_vma=False,
    )
```

```python
import functools
import math

import jax
import jax.numpy as jnp
from jax import lax
from jax.experimental import pallas as pl
from jax.experimental.pallas import tpu as pltpu
from jax.sharding import PartitionSpec as P

MESH = pl.DeviceIdType.MESH
LOGIT_SHARPNESS = 2.0
LOGIT_OFFSET = -2.0

ROUNDS = 3
CHIPS = 32
PIECES = 16
LANES = 128
CHUNKS = 9
FLIGHT = 3
TEXTS_AT = 5
FIRST_AT = 5
SECOND_AT = 7
THIRD_AT = 8
GROUPS = [("y", g) for g in range(9)] + [("x", g) for g in range(9)]


def terms(s):
    logit = LOGIT_SHARPNESS * s + LOGIT_OFFSET
    e = jnp.exp(-jnp.abs(logit))
    weight = jnp.where(logit >= 0.0, 1.0, e) / (1.0 + e)
    loss = jnp.maximum(logit, 0.0) + jnp.log1p(e)
    return logit, weight, loss


def nt(a, b):
    return lax.dot_general(a, b, (((1,), (1,)), ((), ())), preferred_element_type=jnp.float32)


def nn(a, b):
    return jnp.dot(a, b, preferred_element_type=jnp.float32)


def wait_bytes(ref, sem):
    pltpu.make_async_copy(ref, ref, sem).wait()


def kernel(pairs, images_hbm, texts_hbm, positives_hbm, plan_hbm, image_grad, text_grad, totals, *scratch):
    own, rr, stg, arr = (scratch[k * CHUNKS : (k + 1) * CHUNKS] for k in range(4))
    (
        images, texts, pos_row, plan, xb, yb, stat, stat_z, stat_all, stat_sibling, red1, red2,
        load, send1, recv1, sends, recvs, send2, recv2, sendr, recvr, ready,
    ) = scratch[4 * CHUNKS :]
    rows, width = images.shape
    row_groups = rows // 16
    scale = 1.0 / math.sqrt(width)
    factor = LOGIT_SHARPNESS * scale

    dp = lax.axis_index("dp")
    blk = lax.axis_index("blk")
    core = lax.rem(dp, 2)
    chip = dp // 2
    place = (chip // 8) * 4 + lax.rem(chip, 4)

    def piece_of(t):
        return (t // 8) * 4 + lax.rem(t, 4)

    def peer_in_half(m):
        return chip ^ ((m // 4) * 8 + lax.rem(m, 4))

    def along_z(i):
        return dp ^ (2 * lax.rem(i, 8)), blk ^ (4 * (i // 8))

    def across(i):
        return dp ^ (16 * (i // 4)), blk ^ lax.rem(i, 4)

    loads = [
        pltpu.make_async_copy(source, target, load.at[k])
        for k, (source, target) in enumerate(
            [(texts_hbm, texts), (images_hbm, images), (plan_hbm, plan), (positives_hbm, pos_row)]
        )
    ]
    for copy in loads:
        copy.start()

    barrier = pltpu.get_barrier_semaphore()

    def greet(i, carry):
        pl.semaphore_signal(barrier, inc=1, device_id=(2 * (chip ^ i), blk), device_id_type=MESH)
        return carry

    lax.fori_loop(1, CHIPS, greet, 0)

    @pl.when(core == 1)
    def _():
        pl.semaphore_signal(barrier, inc=1, device_id=(dp ^ 1, blk), device_id_type=MESH)

        def greet_z(i, carry):
            pl.semaphore_signal(barrier, inc=1, device_id=along_z(i), device_id_type=MESH)
            return carry

        lax.fori_loop(8, 16, greet_z, 0)

        def greet_across(i, carry):
            other = across((i // 3) * 4 + lax.rem(i, 3) + 1)
            pl.semaphore_signal(barrier, inc=1, device_id=other, device_id_type=MESH)
            return carry

        lax.fori_loop(0, 12, greet_across, 0)

    loads[0].wait()
    yb[...] = texts[...].astype(jnp.bfloat16)
    loads[1].wait()
    xb[...] = images[...].astype(jnp.bfloat16)
    for position, (kind, g) in enumerate(GROUPS):
        source = yb if kind == "y" else xb
        c, side = position // 2, position % 2
        columns = source[:, g * LANES : (g + 1) * LANES]
        own[c][side * row_groups : (side + 1) * row_groups] = columns.reshape(row_groups, 16, LANES)
    for c in range(CHUNKS):
        rr[c][core, chip] = own[c][place]

    @pl.when(core == 0)
    def _():
        pl.semaphore_wait(barrier, 2 * CHIPS - 1)
        pl.semaphore_signal(ready, inc=1, device_id=(dp ^ 1, blk), device_id_type=MESH)

    @pl.when(core == 1)
    def _():
        pl.semaphore_wait(ready, 1)

    def spread(c):
        def send(i, carry):
            t = chip ^ i
            pltpu.make_async_remote_copy(
                src_ref=own[c].at[piece_of(t)],
                dst_ref=rr[c].at[core, chip],
                send_sem=send1.at[c],
                recv_sem=recv1.at[c],
                device_id=(2 * t + core, blk),
                device_id_type=MESH,
            ).start()
            return carry

        lax.fori_loop(1, CHIPS, send, 0)

    for c in range(FLIGHT):
        spread(c)

    loads[3].wait()
    s = nt(xb[...], yb[...]) * scale
    label_t = (lax.broadcasted_iota(jnp.int32, (rows, rows), 0) == pos_row[...]).astype(jnp.float32)
    label = label_t.T
    logit, weight, loss = terms(s)
    weight = weight - label
    loss_sum = loss - label * logit
    weight_sum = weight
    product_sum = weight * s
    image_grad[...] = nn(weight.astype(jnp.bfloat16), yb[...])
    weight = terms(nt(yb[...], xb[...]) * scale)[1] - label_t
    text_grad[...] = nn(weight.astype(jnp.bfloat16), xb[...])

    def deliver(c):
        wait_bytes(rr[c].at[0, pl.ds(0, CHIPS - 1)], recv1.at[c])
        share = pltpu.make_async_remote_copy(
            src_ref=rr[c].at[core],
            dst_ref=rr[c].at[core],
            send_sem=sends.at[c],
            recv_sem=recvs.at[c],
            device_id=(dp ^ 1, blk),
            device_id_type=MESH,
        )
        share.start()
        share.wait_recv()

        for r in range(ROUNDS):
            p = plan[r, dp]
            arr[c][place, r] = rr[c][lax.rem(p, 2), p // 2]

        def send(m, carry):
            t = peer_in_half(m)
            for r in range(ROUNDS):
                p = plan[r, 2 * t + core]
                stg[c][m, r] = rr[c][lax.rem(p, 2), p // 2]
            pltpu.make_async_remote_copy(
                src_ref=stg[c].at[m],
                dst_ref=arr[c].at[place],
                send_sem=send2.at[c],
                recv_sem=recv2.at[c],
                device_id=(2 * t + core, blk),
                device_id_type=MESH,
            ).start()
            return carry

        lax.fori_loop(1, PIECES, send, 0)
        if c + FLIGHT < CHUNKS:
            spread(c + FLIGHT)

    def their(kind, g, r):
        position = GROUPS.index((kind, g))
        c, side = position // 2, position % 2
        return arr[c][side * row_groups : (side + 1) * row_groups, r].reshape(rows, LANES)

    def scores(kind, mine, waited):
        sums = [jnp.zeros((rows, rows), jnp.float32) for _ in range(ROUNDS)]
        for g in range(width // LANES):
            c = GROUPS.index((kind, g)) // 2
            if c not in waited:
                wait_bytes(arr[c].at[pl.ds(0, PIECES - 1)], recv2.at[c])
                waited.add(c)
            for r in range(ROUNDS):
                sums[r] = sums[r] + nt(mine[:, g * LANES : (g + 1) * LANES], their(kind, g, r))
        return sums

    loads[2].wait()
    for c in range(TEXTS_AT + 1):
        deliver(c)

    waited = set()
    weights = []
    for s in scores("y", xb, waited):
        s = s * scale
        logit, weight, loss = terms(s)
        loss_sum = loss_sum + loss
        weight_sum = weight_sum + weight
        product_sum = product_sum + weight * s
        weights.append(weight.astype(jnp.bfloat16))
    lane = lax.broadcasted_iota(jnp.int32, (1, rows), 1)
    stat[...] = jnp.zeros((1, rows), jnp.float32)
    for k, v in enumerate((loss_sum, weight_sum, product_sum)):
        stat[...] += jnp.where(lane == k, jnp.sum(v), 0.0)

    def exchange(k, source, slots, at, peer):
        slots[at] = source[...]

        def send(i, carry):
            pltpu.make_async_remote_copy(
                src_ref=source,
                dst_ref=slots.at[at],
                send_sem=sendr.at[k],
                recv_sem=recvr.at[k],
                device_id=peer(i),
                device_id_type=MESH,
            ).start()
            return carry

        lax.fori_loop(1, 16, send, 0)

    def to_sibling(k, source):
        return pltpu.make_async_remote_copy(
            src_ref=source,
            dst_ref=stat_sibling,
            send_sem=sendr.at[k],
            recv_sem=recvr.at[k],
            device_id=(dp ^ 1, blk),
            device_id_type=MESH,
        )

    @pl.when(core == 0)
    def _():
        to_sibling(2, stat).start()

    for c in range(TEXTS_AT + 1, FIRST_AT + 1):
        deliver(c)

    @pl.when(core == 1)
    def _():
        to_sibling(2, stat).wait_recv()
        stat[...] += stat_sibling[...]
        pl.semaphore_wait(barrier, 8 + 12)
        exchange(0, stat, red1, (blk // 4) * 8 + lax.rem(chip, 8), along_z)

    for c in range(FIRST_AT + 1, SECOND_AT + 1):
        deliver(c)

    @pl.when(core == 1)
    def _():
        wait_bytes(red1.at[pl.ds(0, 15)], recvr.at[0])
        stat_z[...] = jnp.sum(red1[...], axis=0)
        exchange(1, stat_z, red2, (chip // 8) * 4 + lax.rem(blk, 4), across)

    for c in range(SECOND_AT + 1, THIRD_AT + 1):
        deliver(c)

    @pl.when(core == 1)
    def _():
        wait_bytes(red2.at[pl.ds(0, 15)], recvr.at[1])
        stat_all[...] = jnp.sum(red2[...], axis=0)
        stat_sibling[...] = stat_all[...]
        to_sibling(3, stat_all).start()

    for c in range(THIRD_AT + 1, CHUNKS):
        deliver(c)

    for g in range(width // LANES):
        at = slice(g * LANES, (g + 1) * LANES)
        image_sum = image_grad[:, at]
        for r in range(ROUNDS):
            image_sum = image_sum + nn(weights[r], their("y", g, r))
        image_grad[:, at] = image_sum * factor

    weights = [terms(s * scale)[1].astype(jnp.bfloat16) for s in scores("x", yb, waited)]
    for g in range(width // LANES):
        at = slice(g * LANES, (g + 1) * LANES)
        text_sum = text_grad[:, at]
        for r in range(ROUNDS):
            text_sum = text_sum + nn(weights[r], their("x", g, r))
        text_grad[:, at] = text_sum * factor

    @pl.when(core == 0)
    def _():
        to_sibling(3, stat_all).wait_recv()

    total = stat_sibling[...]
    for k in range(3):
        totals[k] = jnp.sum(jnp.where(lane == k, total, 0.0)) / pairs

    for c in range(CHUNKS):
        wait_bytes(rr[c].at[0, pl.ds(0, CHIPS - 1)], send1.at[c])
        wait_bytes(rr[c].at[0], sends.at[c])
        wait_bytes(arr[c].at[pl.ds(0, PIECES - 1)], send2.at[c])

    @pl.when(core == 0)
    def _():
        to_sibling(2, stat).wait_send()

    @pl.when(core == 1)
    def _():
        wait_bytes(red1.at[pl.ds(0, 15)], sendr.at[0])
        wait_bytes(red2.at[pl.ds(0, 15)], sendr.at[1])
        to_sibling(3, stat_all).wait_send()


def body(images, texts, positives, plan):
    rows, width = images.shape
    rounds = plan.shape[0]
    pairs = float(rows * rows * (rounds + 1) * lax.axis_size("dp") * lax.axis_size("blk"))
    vmem = pl.BlockSpec(memory_space=pltpu.VMEM)
    smem = pl.BlockSpec(memory_space=pltpu.SMEM)
    hbm = pl.BlockSpec(memory_space=pltpu.HBM)
    dma = pltpu.SemaphoreType.DMA
    sixteen, single = jnp.bfloat16, jnp.float32
    return pl.pallas_call(
        functools.partial(kernel, pairs),
        out_shape=(
            jax.ShapeDtypeStruct((rows, width), single),
            jax.ShapeDtypeStruct((rows, width), single),
            jax.ShapeDtypeStruct((3,), single),
        ),
        in_specs=[hbm, hbm, hbm, hbm],
        out_specs=(vmem, vmem, smem),
        scratch_shapes=[
            *[pltpu.VMEM((PIECES, 16, LANES), sixteen)] * CHUNKS,
            *[pltpu.VMEM((2, CHIPS, 16, LANES), sixteen)] * CHUNKS,
            *[pltpu.VMEM((PIECES, ROUNDS, 16, LANES), sixteen)] * CHUNKS,
            *[pltpu.VMEM((PIECES, ROUNDS, 16, LANES), sixteen)] * CHUNKS,
            pltpu.VMEM((rows, width), single),
            pltpu.VMEM((rows, width), single),
            pltpu.VMEM((1, rows), jnp.int32),
            pltpu.SMEM(plan.shape, jnp.int32),
            pltpu.VMEM((rows, width), sixteen),
            pltpu.VMEM((rows, width), sixteen),
            *[pltpu.VMEM((1, rows), single)] * 4,
            *[pltpu.VMEM((16, 1, rows), single)] * 2,
            dma((4,)),
            dma((CHUNKS,)), dma((CHUNKS,)),
            dma((CHUNKS,)), dma((CHUNKS,)),
            dma((CHUNKS,)), dma((CHUNKS,)),
            dma((4,)), dma((4,)),
            pltpu.SemaphoreType.REGULAR,
        ],
        compiler_params=pltpu.CompilerParams(
            collective_id=0, has_side_effects=True, vmem_limit_bytes=60 * 1024 * 1024
        ),
        cost_estimate=pl.CostEstimate(flops=600_000_000, bytes_accessed=3_000_000, transcendentals=400_000),
    )(images, texts, positives.reshape(1, rows), plan)


def solution(mesh):
    placed = (P(("dp", "blk"), None), P(("dp", "blk"), None), P(("dp", "blk")), P())
    return jax.shard_map(
        body,
        mesh=mesh,
        in_specs=placed,
        out_specs=(P(("dp", "blk"), None), P(("dp", "blk"), None), P()),
        check_vma=False,
    )
```
